32 devices in a mesh: groups: 2 (over y), seq: 16 (over z, x, core).
Axes of the slice: x: 2, y: 2, z: 4, core: 2. Of those that a mesh axis runs over, the one named last changes fastest.
Arguments:
- query_rows: bfloat16 [6144, 4096], P(('groups', 'seq')), parts along dimension 0, may hold values from -6 to 6
- key_rows: bfloat16 [6144, 512], P(('groups', 'seq')), parts along dimension 0, may hold values from -6 to 6
- value_rows: bfloat16 [6144, 512], P(('groups', 'seq')), parts along dimension 0, may hold values from -6 to 6
- keep_rank: int32 [32, 192], P(('groups', 'seq')), parts along dimension 0, may hold values from 0 to 191, each once within a row
- out_grad: bfloat16 [512, 4096], P(('groups', 'seq')), parts along dimension 0, may hold values from -6 to 6
Outputs:
- attended: bfloat16 [512, 4096], P(('groups', 'seq')), parts along dimension 0
- query_grad: bfloat16 [6144, 4096], P(('groups', 'seq')), parts along dimension 0
- key_grad: bfloat16 [6144, 512], P(('groups', 'seq')), parts along dimension 0
- value_grad: bfloat16 [6144, 512], P(('groups', 'seq')), parts along dimension 0
The draws below stay inside these ranges and needn't reach their ends.
There are 2 independent parts, one for each index of `groups`. The reference program is written for one: setup_inputs(seed, part) draws one part's arguments, and reference() takes and returns one part's arrays. A program takes and returns all parts, laid end to end along the dimension named above; each array names one. Nothing has to cross between parts.
Inputs may be any that keep to these rules, and one draw needn't show every extreme that they name: Each row of keep_rank holds every number 0 to 191 once.
All inputs are finite; a program needn't handle non-finite values.
Results may differ from the reference program's by a relative error of at most 0.025.
Values may be sent and summed in bfloat16 or wider, within the bound.
A program may use at most 64 MiB of HBM per device.

```python
import jax
import jax.numpy as jnp
from jax import lax

HEADS = 32
KVH = 4
HD = 128
VIS_DEV = 192
KEEP_DEV = 16
VIS = 3072
KEPT = 256
N_SEQ = 16


def draw_query_rows(key, part):
    key = jax.random.fold_in(key, 21)
    base_key = jax.random.fold_in(key, 0)
    noise_field = jnp.clip(jax.random.normal(base_key, (VIS, HEADS, HD), jnp.float32), -6.0, 6.0)
    return noise_field.reshape(VIS, HEADS * HD).astype(jnp.bfloat16)


def draw_key_rows(key, part):
    key = jax.random.fold_in(key, 43)
    base_key = jax.random.fold_in(key, 0)
    noise_field = jnp.clip(jax.random.normal(base_key, (VIS, KVH, HD), jnp.float32), -6.0, 6.0)
    return noise_field.reshape(VIS, KVH * HD).astype(jnp.bfloat16)


def level_of(key, extent, cuts, least, largest):
    gain, own = 1.0, jax.random.fold_in(key, 6)
    for dim, blocks in cuts:
        heights = jnp.exp(jax.random.uniform(jax.random.fold_in(own, dim), (blocks,), jnp.float32, least / len(cuts), largest / len(cuts)))
        gain = gain * jnp.repeat(heights, extent[dim] // blocks).reshape([-1 if axis == dim else 1 for axis in range(len(extent))])
    return gain


def noise(key, shape, scale, reach, cuts=(), held_as=jnp.bfloat16):
    level = level_of(key, shape, cuts, -0.22, 0.18) if cuts else 1.0
    entries = jax.random.normal(key, shape, jnp.float32) * scale * level
    return jnp.minimum(jnp.maximum(entries, -reach), reach).astype(held_as)


def setup_inputs(seed: int = 0, part: int = 0) -> dict:
    arg_keys = jax.random.split(jax.random.key(seed), 6)
    own_keys = jax.random.split(jax.random.fold_in(arg_keys[5], part), 6)
    query_rows = draw_query_rows(jax.random.fold_in(jax.random.fold_in(arg_keys[5], part), 71), part)
    key_rows = draw_key_rows(jax.random.fold_in(jax.random.fold_in(arg_keys[5], part), 71), part)
    value_rows = noise(own_keys[2], (VIS, KVH * HD), 1.0, 6.0, ((0, 16),))
    keep_rank = jax.vmap(lambda own: jax.random.permutation(own, VIS_DEV))(jax.random.split(own_keys[3], N_SEQ)).reshape((N_SEQ, VIS_DEV)).astype(jnp.int32)
    out_grad = noise(own_keys[4], (KEPT, HEADS * HD), 1.0, 6.0, ((0, 16),))
    return dict(query_rows=query_rows, key_rows=key_rows, value_rows=value_rows, keep_rank=keep_rank, out_grad=out_grad)


def kept_index(keep_rank):
    shard_total = keep_rank.shape[0]
    block_width = keep_rank.shape[1]
    position = jnp.arange(block_width, dtype=jnp.int32)
    order_key = jnp.where(keep_rank < KEEP_DEV, position[None, :], block_width + position[None, :]).astype(jnp.int32)
    local_rows = jnp.argsort(order_key, axis=1)[:, :KEEP_DEV].astype(jnp.int32)
    base_rows = (jnp.arange(shard_total, dtype=jnp.int32) * block_width)[:, None]
    return (local_rows + base_rows).reshape(-1).astype(jnp.int32)


def one_head(operands):
    query_head, key_head, value_head, grad_head = operands
    score_scale = HD ** -0.5
    seen = jnp.arange(KEPT)[:, None] >= jnp.arange(KEPT)[None, :]
    scores = jnp.dot(query_head, key_head.T, preferred_element_type=jnp.float32) * score_scale
    scores = jnp.where(seen, scores, -jnp.inf)
    row_top = jnp.max(scores, axis=1, keepdims=True)
    exponent = jnp.exp(scores - row_top)
    probs = exponent / jnp.sum(exponent, axis=1, keepdims=True)
    probs_low = probs.astype(jnp.bfloat16)
    attended = jnp.dot(probs_low, value_head, preferred_element_type=jnp.float32).astype(jnp.bfloat16)
    grad_dot = jnp.sum(grad_head.astype(jnp.float32) * attended.astype(jnp.float32), axis=1, keepdims=True)
    grad_prob = jnp.dot(grad_head, value_head.T, preferred_element_type=jnp.float32)
    grad_score = (probs * (grad_prob - grad_dot)).astype(jnp.bfloat16)
    grad_query = (jnp.dot(grad_score, key_head, preferred_element_type=jnp.float32) * score_scale).astype(jnp.bfloat16)
    grad_key = jnp.dot(grad_score.T, query_head, preferred_element_type=jnp.float32) * score_scale
    grad_value = jnp.dot(probs_low.T, grad_head, preferred_element_type=jnp.float32)
    return attended, grad_query, grad_key, grad_value


def reference(query_rows, key_rows, value_rows, keep_rank, out_grad):
    group_size = HEADS // KVH
    kept_rows = kept_index(keep_rank)
    queries = jnp.transpose(query_rows[kept_rows].reshape(KEPT, HEADS, HD), (1, 0, 2))
    keys_kept = jnp.transpose(key_rows[kept_rows].reshape(KEPT, KVH, HD), (1, 0, 2))
    values_kept = jnp.transpose(value_rows[kept_rows].reshape(KEPT, KVH, HD), (1, 0, 2))
    grads = jnp.transpose(out_grad.reshape(KEPT, HEADS, HD), (1, 0, 2))
    keys_rep = jnp.repeat(keys_kept, group_size, axis=0)
    values_rep = jnp.repeat(values_kept, group_size, axis=0)
    attended, grad_query, grad_key, grad_value = lax.map(one_head, (queries, keys_rep, values_rep, grads))
    attended = jnp.transpose(attended, (1, 0, 2)).reshape(KEPT, HEADS * HD)
    grad_query = jnp.transpose(grad_query, (1, 0, 2)).reshape(KEPT, HEADS * HD)
    grad_key = grad_key.reshape(KVH, group_size, KEPT, HD).sum(axis=1)
    grad_value = grad_value.reshape(KVH, group_size, KEPT, HD).sum(axis=1)
    grad_key = jnp.transpose(grad_key, (1, 0, 2)).reshape(KEPT, KVH * HD).astype(jnp.bfloat16)
    grad_value = jnp.transpose(grad_value, (1, 0, 2)).reshape(KEPT, KVH * HD).astype(jnp.bfloat16)
    query_grad = jnp.zeros((VIS, HEADS * HD), jnp.bfloat16).at[kept_rows].set(grad_query)
    key_grad = jnp.zeros((VIS, KVH * HD), jnp.bfloat16).at[kept_rows].set(grad_key)
    value_grad = jnp.zeros((VIS, KVH * HD), jnp.bfloat16).at[kept_rows].set(grad_value)
    return (attended, query_grad, key_grad, value_grad)
```

```python
import functools

import jax
import jax.numpy as jnp
from jax import lax
from jax.experimental import pallas as pl
from jax.experimental.pallas import tpu as pltpu
from jax.sharding import PartitionSpec as P

HEADS = 32
KVH = 4
HD = 128
GROUP = HEADS // KVH
QUAD = KVH
GW = GROUP * HD
CHUNKS = 2
BF = jnp.bfloat16
F32 = jnp.float32
MESH = pl.DeviceIdType.MESH


def dot(a, b, ca, cb):
    return lax.dot_general(a, b, (((ca,), (cb,)), ((), ())), preferred_element_type=F32)


def kernel(
    n, keep, q_hbm, k_hbm, v_hbm, rank_ref, g_hbm, att_out, dq_out, dk_out, dv_out,
    q_in, k_in, v_in, g_in, q_send, g_send, kv_send, q_recv, g_recv, kv_recv,
    dkv_send, dkv_recv, att_send, dqs_send, att_recv, dqs_recv, dq_full, dk_full, dv_full,
    dk_acc, dv_acc, in_sem, out_sem, qg_ssem, qg_rsem, kv_ssem, kv_rsem,
    ad_ssem, ad_rsem, dkv_ssem, dkv_rsem,
):
    rows = q_in.shape[0]
    me = lax.axis_index("seq")
    quad = me // QUAD
    mine = me % QUAD
    base = quad * QUAD
    keys = n * keep
    scale = HD ** -0.5

    loads = []
    for i, (src, dst) in enumerate(((k_hbm, k_in), (v_hbm, v_in), (g_hbm, g_in), (q_hbm, q_in))):
        cp = pltpu.make_async_copy(src, dst, in_sem.at[i])
        cp.start()
        loads.append(cp)

    barrier = pltpu.get_barrier_semaphore()

    def greet(off, c):
        pl.semaphore_signal(
            barrier, inc=1, device_id={"seq": lax.rem(me + off, n)}, device_id_type=MESH
        )
        return c

    lax.fori_loop(1, n, greet, 0)

    def remote(src, dst, ssem, rsem, target):
        return pltpu.make_async_remote_copy(
            src_ref=src, dst_ref=dst, send_sem=ssem, recv_sem=rsem,
            device_id={"seq": target}, device_id_type=MESH,
        )

    chosen = rank_ref[...] < keep
    chosen_low = jnp.broadcast_to(jnp.where(chosen, 1.0, 0.0).astype(F32), (8, rows)).astype(BF)
    upto = (
        lax.broadcasted_iota(jnp.int32, (rows, rows), 0)
        <= lax.broadcasted_iota(jnp.int32, (rows, rows), 1)
    )
    slots = dot(chosen_low, jnp.where(upto, 1.0, 0.0).astype(BF), 1, 0)[0:1]
    slots = jnp.where(chosen, slots, 0.0)
    wanted = lax.broadcasted_iota(jnp.int32, (keep, rows), 0).astype(F32) + 1.0
    sel = jnp.where(wanted == slots, 1.0, 0.0).astype(BF)

    loads[0].wait()
    loads[1].wait()
    k_kept = dot(sel, k_in[...], 1, 0).astype(BF)
    v_kept = dot(sel, v_in[...], 1, 0).astype(BF)
    for g in range(KVH):
        kv_send[g, :, :HD] = k_kept[:, g * HD:(g + 1) * HD]
        kv_send[g, :, HD:] = v_kept[:, g * HD:(g + 1) * HD]
    kv_recv[me] = kv_send[mine]

    def clear(s, c):
        kv_recv[s] = jnp.zeros((keep, 2 * HD), BF)
        return c

    lax.fori_loop(base + QUAD, n, clear, 0)

    loads[2].wait()
    for h in range(HEADS):
        g_send[h] = g_in[:, h * HD:(h + 1) * HD]

    pl.semaphore_wait(barrier, n - 1)

    def kv_copy(target, source):
        return remote(
            kv_send.at[target % QUAD], kv_recv.at[source], kv_ssem.at[target],
            kv_rsem.at[source], target,
        )

    def qg_copy(which, d, send):
        peer = (mine + d) % QUAD
        buf_s, buf_r = ((q_send, q_recv), (g_send, g_recv))[which]
        return remote(
            buf_s.at[pl.ds(peer * GROUP, GROUP)], buf_r.at[:, mine if send else peer],
            qg_ssem.at[which, d], qg_rsem.at[which, mine if send else peer], base + peer,
        )

    def send_kv(i, c):
        target = n - 1 - i

        @pl.when(target != me)
        def _():
            kv_copy(target, me).start()

        return c

    lax.fori_loop(0, n - base, send_kv, 0)
    for d in (2, 3, 1):
        qg_copy(1, d, True).start()

    loads[3].wait()
    for d in (2, 3, 1, 0):
        peer = (mine + d) % QUAD
        cols = pl.ds(pl.multiple_of(peer * GW, GW), GW)
        part = dot(sel, q_in[:, cols], 1, 0).astype(BF)
        for h in range(GROUP):
            if d == 0:
                q_recv[h, mine] = part[:, h * HD:(h + 1) * HD]
            else:
                q_send[peer * GROUP + h] = part[:, h * HD:(h + 1) * HD]
        if d != 0:
            qg_copy(0, d, True).start()
    for h in range(GROUP):
        g_recv[h, mine] = g_send[mine * GROUP + h]

    def wait_kv(s, c):
        @pl.when(s != me)
        def _():
            kv_copy(s, s).wait_recv()

        return c

    lax.fori_loop(0, base + QUAD, wait_kv, 0)
    for d in (1, 2, 3):
        qg_copy(1, d, False).wait_recv()
    for d in (1, 2, 3):
        qg_copy(0, d, False).wait_recv()

    kv = kv_recv[...].reshape(keys, 2 * HD)
    k_all, v_all = kv[:, :HD], kv[:, HD:]
    span = QUAD * keep
    hc = GROUP // CHUNKS
    crows = hc * span
    row_pos = base * keep + lax.broadcasted_iota(jnp.int32, (crows, keys), 0) % span
    seen = row_pos >= lax.broadcasted_iota(jnp.int32, (crows, keys), 1)

    def ad_copy(which, chunk, d, send):
        peer = (mine + d) % QUAD
        buf_s, buf_r = ((att_send, att_recv), (dqs_send, dqs_recv))[which]
        slot = mine if send else peer
        cols = pl.ds(chunk * hc * HD, hc * HD)
        return remote(
            buf_s.at[peer, :, cols], buf_r.at[slot, :, cols],
            ad_ssem.at[which, chunk, d], ad_rsem.at[which, chunk, slot], base + peer,
        )

    for c in range(CHUNKS):
        q_c = q_recv[c * hc:(c + 1) * hc].reshape(crows, HD)
        g_c = g_recv[c * hc:(c + 1) * hc].reshape(crows, HD)
        scores = jnp.where(seen, dot(q_c, k_all, 1, 1) * scale, -jnp.inf)
        top = jnp.max(scores, axis=1, keepdims=True)
        e = jnp.exp(scores - top)
        probs = e * (1.0 / jnp.sum(e, axis=1, keepdims=True))
        low = probs.astype(BF)
        att = dot(low, v_all, 1, 0).astype(BF)
        gdot = jnp.sum(g_c.astype(F32) * att.astype(F32), axis=1, keepdims=True)
        gprob = dot(g_c, v_all, 1, 1)
        ds = (probs * (gprob - gdot)).astype(BF)
        dq = (dot(ds, k_all, 1, 0) * scale).astype(BF)
        for h in range(hc):
            hcol = slice((c * hc + h) * HD, (c * hc + h + 1) * HD)
            for b in range(QUAD):
                r0 = h * span + b * keep
                att_send[b, :, hcol] = att[r0:r0 + keep]
                dqs_send[b, :, hcol] = dq[r0:r0 + keep]
        for d in (2, 3, 1):
            for w in (0, 1):
                ad_copy(w, c, d, True).start()
        dk_part = dot(ds, q_c, 0, 0)
        dv_part = dot(low, g_c, 0, 0)
        if c == 0:
            dk_acc[...] = dk_part
            dv_acc[...] = dv_part
        else:
            dk_acc[...] += dk_part
            dv_acc[...] += dv_part

    dkv_send[:, :, :HD] = (dk_acc[...] * scale).astype(BF).reshape(n, keep, HD)
    dkv_send[:, :, HD:] = dv_acc[...].astype(BF).reshape(n, keep, HD)

    def dkv_copy(target, source):
        return remote(
            dkv_send.at[target], dkv_recv.at[source], dkv_ssem.at[target],
            dkv_rsem.at[source], target,
        )

    def send_dkv(t, c):
        @pl.when(t != me)
        def _():
            dkv_copy(t, me).start()

        return c

    lax.fori_loop(0, base + QUAD, send_dkv, 0)
    dkv_recv[me] = dkv_send[me]
    att_recv[mine] = att_send[mine]
    dqs_recv[mine] = dqs_send[mine]

    for d in (0, 1, 3, 2):
        peer = (mine + d) % QUAD
        cols = pl.ds(pl.multiple_of(peer * GW, GW), GW)
        if d:
            for c in range(CHUNKS):
                ad_copy(0, c, d, False).wait_recv()
                ad_copy(1, c, d, False).wait_recv()
        pltpu.make_async_copy(att_recv.at[peer], att_out.at[:, cols], out_sem.at[0, d]).start()
        dq_full[:, cols] = dot(sel, dqs_recv[peer], 0, 0).astype(BF)
        pltpu.make_async_copy(dq_full.at[:, cols], dq_out.at[:, cols], out_sem.at[1, d]).start()

    def wait_dkv(s, c):
        @pl.when(s != me)
        def _():
            dkv_copy(s, s).wait_recv()

        return c

    lax.fori_loop(base, n, wait_dkv, 0)

    def add_quad(j, tot):
        return tuple(
            tot[g] + dkv_recv[j * QUAD + g].astype(F32) for g in range(KVH)
        )

    total = lax.fori_loop(
        quad, n // QUAD, add_quad, tuple(jnp.zeros((keep, 2 * HD), F32) for _ in range(KVH))
    )
    dk_kept = jnp.concatenate([t[:, :HD] for t in total], axis=1).astype(BF)
    dv_kept = jnp.concatenate([t[:, HD:] for t in total], axis=1).astype(BF)
    dk_full[...] = dot(sel, dk_kept, 0, 0).astype(BF)
    dv_full[...] = dot(sel, dv_kept, 0, 0).astype(BF)
    last = [
        pltpu.make_async_copy(dk_full, dk_out, out_sem.at[2, 0]),
        pltpu.make_async_copy(dv_full, dv_out, out_sem.at[2, 1]),
    ]
    for cp in last:
        cp.start()

    def drain_kv(t, c):
        @pl.when(t != me)
        def _():
            kv_copy(t, me).wait_send()

        return c

    lax.fori_loop(base, n, drain_kv, 0)

    def drain_dkv(t, c):
        @pl.when(t != me)
        def _():
            dkv_copy(t, me).wait_send()

        return c

    lax.fori_loop(0, base + QUAD, drain_dkv, 0)
    for d in (1, 2, 3):
        for w in (0, 1):
            qg_copy(w, d, True).wait_send()
            for c in range(CHUNKS):
                ad_copy(w, c, d, True).wait_send()
    for d in range(QUAD):
        peer = (mine + d) % QUAD
        cols = pl.ds(pl.multiple_of(peer * GW, GW), GW)
        pltpu.make_async_copy(att_recv.at[peer], att_out.at[:, cols], out_sem.at[0, d]).wait()
        pltpu.make_async_copy(dq_full.at[:, cols], dq_out.at[:, cols], out_sem.at[1, d]).wait()
    for cp in last:
        cp.wait()


def body(query_rows, key_rows, value_rows, keep_rank, out_grad):
    n = lax.axis_size("seq")
    rows = query_rows.shape[0]
    keep = out_grad.shape[0]
    width = HEADS * HD
    kvw = KVH * HD
    any_spec = pl.BlockSpec(memory_space=pl.ANY)
    vmem = pl.BlockSpec(memory_space=pltpu.VMEM)
    dma = pltpu.SemaphoreType.DMA
    return pl.pallas_call(
        functools.partial(kernel, n, keep),
        out_shape=(
            jax.ShapeDtypeStruct((keep, width), BF),
            jax.ShapeDtypeStruct((rows, width), BF),
            jax.ShapeDtypeStruct((rows, kvw), BF),
            jax.ShapeDtypeStruct((rows, kvw), BF),
        ),
        in_specs=[any_spec, any_spec, any_spec, vmem, any_spec],
        out_specs=(any_spec,) * 4,
        scratch_shapes=[
            pltpu.VMEM((rows, width), BF),
            pltpu.VMEM((rows, kvw), BF),
            pltpu.VMEM((rows, kvw), BF),
            pltpu.VMEM((keep, width), BF),
            pltpu.VMEM((HEADS, keep, HD), BF),
            pltpu.VMEM((HEADS, keep, HD), BF),
            pltpu.VMEM((KVH, keep, 2 * HD), BF),
            pltpu.VMEM((GROUP, QUAD, keep, HD), BF),
            pltpu.VMEM((GROUP, QUAD, keep, HD), BF),
            pltpu.VMEM((n, keep, 2 * HD), BF),
            pltpu.VMEM((n, keep, 2 * HD), BF),
            pltpu.VMEM((n, keep, 2 * HD), BF),
            pltpu.VMEM((QUAD, keep, GW), BF),
            pltpu.VMEM((QUAD, keep, GW), BF),
            pltpu.VMEM((QUAD, keep, GW), BF),
            pltpu.VMEM((QUAD, keep, GW), BF),
            pltpu.VMEM((rows, width), BF),
            pltpu.VMEM((rows, kvw), BF),
            pltpu.VMEM((rows, kvw), BF),
            pltpu.VMEM((n * keep, HD), F32),
            pltpu.VMEM((n * keep, HD), F32),
            dma((4,)),
            dma((3, QUAD)),
            dma((2, QUAD)),
            dma((2, QUAD)),
            dma((n,)),
            dma((n,)),
            dma((2, CHUNKS, QUAD)),
            dma((2, CHUNKS, QUAD)),
            dma((n,)),
            dma((n,)),
        ],
        compiler_params=pltpu.CompilerParams(
            collective_id=0, has_side_effects=True, vmem_limit_bytes=48 * 1024 * 1024
        ),
    )(query_rows, key_rows, value_rows, keep_rank, out_grad)


def solution(mesh):
    spec = P(("groups", "seq"), None)
    return jax.shard_map(
        body, mesh=mesh, in_specs=(spec,) * 5, out_specs=(spec,) * 4, check_vma=False
    )
```

```python
import functools

import jax
import jax.numpy as jnp
from jax import lax
from jax.experimental import pallas as pl
from jax.experimental.pallas import tpu as pltpu
from jax.sharding import PartitionSpec as P

HEADS = 32
KVH = 4
HD = 128
GROUP = HEADS // KVH
QUAD = KVH
GW = GROUP * HD
CHUNKS = 2
BF = jnp.bfloat16
F32 = jnp.float32
MESH = pl.DeviceIdType.MESH


def dot(a, b, ca, cb):
    return lax.dot_general(a, b, (((ca,), (cb,)), ((), ())), preferred_element_type=F32)


def kernel(
    n, keep, q_hbm, k_hbm, v_hbm, rank_ref, g_hbm, att_out, dq_out, dkv_out, sel_out,
    q_in, k_in, v_in, g_in, q_send, g_send, kv_send, q_recv, g_recv, kv_recv,
    dkv_send, dkv_recv, att_send, dqs_send, att_recv, dqs_recv, dkv_kept, sel_keep,
    dk_acc, dv_acc, in_sem, out_sem, qg_ssem, qg_rsem, kv_ssem, kv_rsem,
    ad_ssem, ad_rsem, dkv_ssem, dkv_rsem,
):
    rows = q_in.shape[0]
    me = lax.axis_index("seq")
    quad = me // QUAD
    mine = me % QUAD
    base = quad * QUAD
    keys = n * keep
    scale = HD ** -0.5

    loads = []
    for i, (src, dst) in enumerate(((k_hbm, k_in), (v_hbm, v_in), (g_hbm, g_in), (q_hbm, q_in))):
        cp = pltpu.make_async_copy(src, dst, in_sem.at[i])
        cp.start()
        loads.append(cp)

    barrier = pltpu.get_barrier_semaphore()

    def greet(off, c):
        pl.semaphore_signal(
            barrier, inc=1, device_id={"seq": lax.rem(me + off, n)}, device_id_type=MESH
        )
        return c

    lax.fori_loop(1, n, greet, 0)

    def remote(src, dst, ssem, rsem, target):
        return pltpu.make_async_remote_copy(
            src_ref=src, dst_ref=dst, send_sem=ssem, recv_sem=rsem,
            device_id={"seq": target}, device_id_type=MESH,
        )

    chosen = rank_ref[...] < keep
    chosen_low = jnp.broadcast_to(jnp.where(chosen, 1.0, 0.0).astype(F32), (8, rows)).astype(BF)
    upto = (
        lax.broadcasted_iota(jnp.int32, (rows, rows), 0)
        <= lax.broadcasted_iota(jnp.int32, (rows, rows), 1)
    )
    slots = dot(chosen_low, jnp.where(upto, 1.0, 0.0).astype(BF), 1, 0)[0:1]
    slots = jnp.where(chosen, slots, 0.0)
    wanted = lax.broadcasted_iota(jnp.int32, (keep, rows), 0).astype(F32) + 1.0
    sel = jnp.where(wanted == slots, 1.0, 0.0).astype(BF)
    sel_keep[...] = sel
    sel_copy = pltpu.make_async_copy(sel_keep, sel_out, out_sem.at[2, 0])
    sel_copy.start()

    loads[0].wait()
    loads[1].wait()
    k_kept = dot(sel, k_in[...], 1, 0).astype(BF)
    v_kept = dot(sel, v_in[...], 1, 0).astype(BF)
    for g in range(KVH):
        kv_send[g, :, :HD] = k_kept[:, g * HD:(g + 1) * HD]
        kv_send[g, :, HD:] = v_kept[:, g * HD:(g + 1) * HD]
    kv_recv[me] = kv_send[mine]

    def clear(s, c):
        kv_recv[s] = jnp.zeros((keep, 2 * HD), BF)
        return c

    lax.fori_loop(base + QUAD, n, clear, 0)

    loads[2].wait()
    for h in range(HEADS):
        g_send[h] = g_in[:, h * HD:(h + 1) * HD]

    pl.semaphore_wait(barrier, n - 1)

    def kv_copy(target, source):
        return remote(
            kv_send.at[target % QUAD], kv_recv.at[source], kv_ssem.at[target],
            kv_rsem.at[source], target,
        )

    def qg_copy(which, d, send):
        peer = (mine + d) % QUAD
        buf_s, buf_r = ((q_send, q_recv), (g_send, g_recv))[which]
        return remote(
            buf_s.at[pl.ds(peer * GROUP, GROUP)], buf_r.at[:, mine if send else peer],
            qg_ssem.at[which, d], qg_rsem.at[which, mine if send else peer], base + peer,
        )

    def send_kv(i, c):
        target = n - 1 - i

        @pl.when(target != me)
        def _():
            kv_copy(target, me).start()

        return c

    lax.fori_loop(0, n - base, send_kv, 0)
    for d in (2, 3, 1):
        qg_copy(1, d, True).start()

    loads[3].wait()
    for d in (2, 3, 1, 0):
        peer = (mine + d) % QUAD
        cols = pl.ds(pl.multiple_of(peer * GW, GW), GW)
        part = dot(sel, q_in[:, cols], 1, 0).astype(BF)
        for h in range(GROUP):
            if d == 0:
                q_recv[h, mine] = part[:, h * HD:(h + 1) * HD]
            else:
                q_send[peer * GROUP + h] = part[:, h * HD:(h + 1) * HD]
        if d != 0:
            qg_copy(0, d, True).start()
    for h in range(GROUP):
        g_recv[h, mine] = g_send[mine * GROUP + h]

    def wait_kv(s, c):
        @pl.when(s != me)
        def _():
            kv_copy(s, s).wait_recv()

        return c

    lax.fori_loop(0, base + QUAD, wait_kv, 0)
    for d in (1, 2, 3):
        qg_copy(1, d, False).wait_recv()
    for d in (1, 2, 3):
        qg_copy(0, d, False).wait_recv()

    kv = kv_recv[...].reshape(keys, 2 * HD)
    k_all, v_all = kv[:, :HD], kv[:, HD:]
    span = QUAD * keep
    hc = GROUP // CHUNKS
    crows = hc * span
    row_pos = base * keep + lax.broadcasted_iota(jnp.int32, (crows, keys), 0) % span
    seen = row_pos >= lax.broadcasted_iota(jnp.int32, (crows, keys), 1)

    def ad_copy(which, chunk, d, send):
        peer = (mine + d) % QUAD
        buf_s, buf_r = ((att_send, att_recv), (dqs_send, dqs_recv))[which]
        slot = mine if send else peer
        cols = pl.ds(chunk * hc * HD, hc * HD)
        return remote(
            buf_s.at[peer, :, cols], buf_r.at[slot, :, cols],
            ad_ssem.at[which, chunk, d], ad_rsem.at[which, chunk, slot], base + peer,
        )

    for c in range(CHUNKS):
        q_c = q_recv[c * hc:(c + 1) * hc].reshape(crows, HD)
        g_c = g_recv[c * hc:(c + 1) * hc].reshape(crows, HD)
        scores = jnp.where(seen, dot(q_c, k_all, 1, 1) * scale, -jnp.inf)
        top = jnp.max(scores, axis=1, keepdims=True)
        e = jnp.exp(scores - top)
        probs = e * (1.0 / jnp.sum(e, axis=1, keepdims=True))
        low = probs.astype(BF)
        att = dot(low, v_all, 1, 0).astype(BF)
        gdot = jnp.sum(g_c.astype(F32) * att.astype(F32), axis=1, keepdims=True)
        gprob = dot(g_c, v_all, 1, 1)
        ds = (probs * (gprob - gdot)).astype(BF)
        dq = (dot(ds, k_all, 1, 0) * scale).astype(BF)
        for h in range(hc):
            hcol = slice((c * hc + h) * HD, (c * hc + h + 1) * HD)
            for b in range(QUAD):
                r0 = h * span + b * keep
                att_send[b, :, hcol] = att[r0:r0 + keep]
                dqs_send[b, :, hcol] = dq[r0:r0 + keep]
        for d in (2, 3, 1):
            for w in (0, 1):
                ad_copy(w, c, d, True).start()
        dk_part = dot(ds, q_c, 0, 0)
        dv_part = dot(low, g_c, 0, 0)
        if c == 0:
            dk_acc[...] = dk_part
            dv_acc[...] = dv_part
        else:
            dk_acc[...] += dk_part
            dv_acc[...] += dv_part

    dkv_send[:, :, :HD] = (dk_acc[...] * scale).astype(BF).reshape(n, keep, HD)
    dkv_send[:, :, HD:] = dv_acc[...].astype(BF).reshape(n, keep, HD)

    def dkv_copy(target, source):
        return remote(
            dkv_send.at[target], dkv_recv.at[source], dkv_ssem.at[target],
            dkv_rsem.at[source], target,
        )

    def send_dkv(t, c):
        @pl.when(t != me)
        def _():
            dkv_copy(t, me).start()

        return c

    lax.fori_loop(0, base + QUAD, send_dkv, 0)
    dkv_recv[me] = dkv_send[me]
    att_recv[mine] = att_send[mine]
    dqs_recv[mine] = dqs_send[mine]

    for d in (0, 1, 3, 2):
        peer = (mine + d) % QUAD
        cols = pl.ds(pl.multiple_of(peer * GW, GW), GW)
        if d:
            for c in range(CHUNKS):
                ad_copy(0, c, d, False).wait_recv()
                ad_copy(1, c, d, False).wait_recv()
        pltpu.make_async_copy(att_recv.at[peer], att_out.at[:, cols], out_sem.at[0, d]).start()
        pltpu.make_async_copy(dqs_recv.at[peer], dq_out.at[:, cols], out_sem.at[1, d]).start()

    def wait_dkv(s, c):
        @pl.when(s != me)
        def _():
            dkv_copy(s, s).wait_recv()

        return c

    lax.fori_loop(base, n, wait_dkv, 0)

    def add_quad(j, tot):
        return tuple(
            tot[g] + dkv_recv[j * QUAD + g].astype(F32) for g in range(KVH)
        )

    total = lax.fori_loop(
        quad, n // QUAD, add_quad, tuple(jnp.zeros((keep, 2 * HD), F32) for _ in range(KVH))
    )
    for g in range(KVH):
        dkv_kept[:, g * HD:(g + 1) * HD] = total[g][:, :HD].astype(BF)
        dkv_kept[:, (KVH + g) * HD:(KVH + g + 1) * HD] = total[g][:, HD:].astype(BF)
    last = [sel_copy, pltpu.make_async_copy(dkv_kept, dkv_out, out_sem.at[2, 1])]
    last[1].start()

    def drain_kv(t, c):
        @pl.when(t != me)
        def _():
            kv_copy(t, me).wait_send()

        return c

    lax.fori_loop(base, n, drain_kv, 0)

    def drain_dkv(t, c):
        @pl.when(t != me)
        def _():
            dkv_copy(t, me).wait_send()

        return c

    lax.fori_loop(0, base + QUAD, drain_dkv, 0)
    for d in (1, 2, 3):
        for w in (0, 1):
            qg_copy(w, d, True).wait_send()
            for c in range(CHUNKS):
                ad_copy(w, c, d, True).wait_send()
    for d in range(QUAD):
        peer = (mine + d) % QUAD
        cols = pl.ds(pl.multiple_of(peer * GW, GW), GW)
        pltpu.make_async_copy(att_recv.at[peer], att_out.at[:, cols], out_sem.at[0, d]).wait()
        pltpu.make_async_copy(dqs_recv.at[peer], dq_out.at[:, cols], out_sem.at[1, d]).wait()
    for cp in last:
        cp.wait()


def spread_kernel(
    att_in, dq_in, dkv_in, sel_in, att_out, dq_out, dk_out, dv_out,
    dq_kept, dkv_kept, sel_ref, dq_full, dk_full, dv_full, in_sem, out_sem,
):
    kvw = KVH * HD
    loads = []
    for i, (src, dst) in enumerate(
        ((sel_in, sel_ref), (dq_in, dq_kept), (dkv_in, dkv_kept), (att_in, att_out))
    ):
        cp = pltpu.make_async_copy(src, dst, in_sem.at[i])
        cp.start()
        loads.append(cp)
    loads[0].wait()
    loads[1].wait()
    sel = sel_ref[...]
    stores = []
    for i in range(QUAD):
        cols = slice(i * GW, (i + 1) * GW)
        dq_full[:, cols] = dot(sel, dq_kept[:, cols], 0, 0).astype(BF)
        stores.append(pltpu.make_async_copy(dq_full.at[:, cols], dq_out.at[:, cols], out_sem.at[i]))
        stores[-1].start()
    loads[2].wait()
    for i, (full, out) in enumerate(((dk_full, dk_out), (dv_full, dv_out))):
        full[...] = dot(sel, dkv_kept[:, i * kvw:(i + 1) * kvw], 0, 0).astype(BF)
        stores.append(pltpu.make_async_copy(full, out, out_sem.at[QUAD + i]))
        stores[-1].start()
    loads[3].wait()
    for cp in stores:
        cp.wait()


def body(query_rows, key_rows, value_rows, keep_rank, out_grad):
    n = lax.axis_size("seq")
    rows = query_rows.shape[0]
    keep = out_grad.shape[0]
    width = HEADS * HD
    kvw = KVH * HD
    any_spec = pl.BlockSpec(memory_space=pl.ANY)
    vmem = pl.BlockSpec(memory_space=pltpu.VMEM)
    dma = pltpu.SemaphoreType.DMA
    hbm = pl.BlockSpec(memory_space=pltpu.HBM)
    att, dq_kept, dkv_kept, sel = pl.pallas_call(
        functools.partial(kernel, n, keep),
        out_shape=(
            jax.ShapeDtypeStruct((keep, width), BF),
            jax.ShapeDtypeStruct((keep, width), BF),
            jax.ShapeDtypeStruct((keep, 2 * kvw), BF),
            jax.ShapeDtypeStruct((keep, rows), BF),
        ),
        in_specs=[hbm, hbm, hbm, vmem, hbm],
        out_specs=(any_spec,) * 4,
        scratch_shapes=[
            pltpu.VMEM((rows, width), BF),
            pltpu.VMEM((rows, kvw), BF),
            pltpu.VMEM((rows, kvw), BF),
            pltpu.VMEM((keep, width), BF),
            pltpu.VMEM((HEADS, keep, HD), BF),
            pltpu.VMEM((HEADS, keep, HD), BF),
            pltpu.VMEM((KVH, keep, 2 * HD), BF),
            pltpu.VMEM((GROUP, QUAD, keep, HD), BF),
            pltpu.VMEM((GROUP, QUAD, keep, HD), BF),
            pltpu.VMEM((n, keep, 2 * HD), BF),
            pltpu.VMEM((n, keep, 2 * HD), BF),
            pltpu.VMEM((n, keep, 2 * HD), BF),
            pltpu.VMEM((QUAD, keep, GW), BF),
            pltpu.VMEM((QUAD, keep, GW), BF),
            pltpu.VMEM((QUAD, keep, GW), BF),
            pltpu.VMEM((QUAD, keep, GW), BF),
            pltpu.VMEM((keep, 2 * kvw), BF),
            pltpu.VMEM((keep, rows), BF),
            pltpu.VMEM((n * keep, HD), F32),
            pltpu.VMEM((n * keep, HD), F32),
            dma((4,)),
            dma((3, QUAD)),
            dma((2, QUAD)),
            dma((2, QUAD)),
            dma((n,)),
            dma((n,)),
            dma((2, CHUNKS, QUAD)),
            dma((2, CHUNKS, QUAD)),
            dma((n,)),
            dma((n,)),
        ],
        compiler_params=pltpu.CompilerParams(
            collective_id=0, has_side_effects=True, vmem_limit_bytes=64 * 1024 * 1024
        ),
    )(query_rows, key_rows, value_rows, keep_rank, out_grad)
    return pl.pallas_call(
        spread_kernel,
        out_shape=(
            jax.ShapeDtypeStruct((keep, width), BF),
            jax.ShapeDtypeStruct((rows, width), BF),
            jax.ShapeDtypeStruct((rows, kvw), BF),
            jax.ShapeDtypeStruct((rows, kvw), BF),
        ),
        in_specs=[any_spec] * 4,
        out_specs=(hbm,) * 4,
        scratch_shapes=[
            pltpu.VMEM((keep, width), BF),
            pltpu.VMEM((keep, 2 * kvw), BF),
            pltpu.VMEM((keep, rows), BF),
            pltpu.VMEM((rows, width), BF),
            pltpu.VMEM((rows, kvw), BF),
            pltpu.VMEM((rows, kvw), BF),
            dma((4,)),
            dma((QUAD + 2,)),
        ],
        compiler_params=pltpu.CompilerParams(vmem_limit_bytes=64 * 1024 * 1024),
    )(att, dq_kept, dkv_kept, sel)


def solution(mesh):
    spec = P(("groups", "seq"), None)
    return jax.shard_map(
        body, mesh=mesh, in_specs=(spec,) * 5, out_specs=(spec,) * 4, check_vma=False
    )
```

```python
import functools

import jax
import jax.numpy as jnp
from jax import lax
from jax.experimental import pallas as pl
from jax.experimental.pallas import tpu as pltpu
from jax.sharding import PartitionSpec as P

HEADS = 32
KVH = 4
HD = 128
GROUP = HEADS // KVH
QUAD = KVH
GW = GROUP * HD
CHUNKS = 2
BF = jnp.bfloat16
F32 = jnp.float32
MESH = pl.DeviceIdType.MESH


def dot(a, b, ca, cb):
    return lax.dot_general(a, b, (((ca,), (cb,)), ((), ())), preferred_element_type=F32)


def kernel(
    n, keep, q_hbm, k_hbm, v_hbm, rank_ref, g_hbm, att_out, dq_out, dkv_out, sel_out,
    q_in, k_in, v_in, g_in, q_send, g_send, kv_send, q_recv, g_recv, kv_recv,
    dkv_send, dkv_recv, att_send, dqs_send, att_recv, dqs_recv, dkv_kept, sel_keep,
    dk_acc, dv_acc, in_sem, out_sem, qg_ssem, qg_rsem, kv_ssem, kv_rsem,
    ad_ssem, ad_rsem, dkv_ssem, dkv_rsem,
):
    rows = q_in.shape[0]
    me = lax.axis_index("seq")
    quad = me // QUAD
    mine = me % QUAD
    base = quad * QUAD
    keys = n * keep
    scale = HD ** -0.5
    hc = GROUP // CHUNKS
    span = QUAD * keep

    def peer_of(d):
        return (mine // 2 + d // 2) % 2 * 2 + (mine + d) % 2

    loads = []
    for i, (src, dst) in enumerate(((k_hbm, k_in), (v_hbm, v_in), (g_hbm, g_in), (q_hbm, q_in))):
        cp = pltpu.make_async_copy(src, dst, in_sem.at[i])
        cp.start()
        loads.append(cp)

    barrier = pltpu.get_barrier_semaphore()

    def greet(off, c):
        pl.semaphore_signal(
            barrier, inc=1, device_id={"seq": lax.rem(me + off, n)}, device_id_type=MESH
        )
        return c

    lax.fori_loop(1, n, greet, 0)

    def remote(src, dst, ssem, rsem, target):
        return pltpu.make_async_remote_copy(
            src_ref=src, dst_ref=dst, send_sem=ssem, recv_sem=rsem,
            device_id={"seq": target}, device_id_type=MESH,
        )

    chosen = rank_ref[...] < keep
    chosen_low = jnp.broadcast_to(jnp.where(chosen, 1.0, 0.0).astype(F32), (8, rows)).astype(BF)
    upto = (
        lax.broadcasted_iota(jnp.int32, (rows, rows), 0)
        <= lax.broadcasted_iota(jnp.int32, (rows, rows), 1)
    )
    slots = dot(chosen_low, jnp.where(upto, 1.0, 0.0).astype(BF), 1, 0)[0:1]
    slots = jnp.where(chosen, slots, 0.0)
    wanted = lax.broadcasted_iota(jnp.int32, (keep, rows), 0).astype(F32) + 1.0
    sel = jnp.where(wanted == slots, 1.0, 0.0).astype(BF)
    sel_keep[...] = sel
    sel_copy = pltpu.make_async_copy(sel_keep, sel_out, out_sem.at[2, 0])
    sel_copy.start()

    loads[0].wait()
    loads[1].wait()
    k_kept = dot(sel, k_in[...], 1, 0).astype(BF)
    v_kept = dot(sel, v_in[...], 1, 0).astype(BF)
    for g in range(KVH):
        kv_send[g, :, :HD] = k_kept[:, g * HD:(g + 1) * HD]
        kv_send[g, :, HD:] = v_kept[:, g * HD:(g + 1) * HD]
    kv_recv[me] = kv_send[mine]

    def clear(s, c):
        kv_recv[s] = jnp.zeros((keep, 2 * HD), BF)
        return c

    lax.fori_loop(base + QUAD, n, clear, 0)

    loads[2].wait()
    for h in range(HEADS):
        g_send[h] = g_in[:, h * HD:(h + 1) * HD]

    pl.semaphore_wait(barrier, n - 1)

    def kv_copy(target, source):
        return remote(
            kv_send.at[target % QUAD], kv_recv.at[source], kv_ssem.at[target],
            kv_rsem.at[source], target,
        )

    def qg_copy(which, c, d, send):
        peer = peer_of(d)
        buf_s, buf_r = ((q_send, q_recv), (g_send, g_recv))[which]
        return remote(
            buf_s.at[pl.ds(peer * GROUP + c * hc, hc)],
            buf_r.at[pl.ds(c * hc, hc), mine if send else peer],
            qg_ssem.at[which, c, d], qg_rsem.at[which, c, mine if send else peer], base + peer,
        )

    def send_kv(i, c):
        target = n - 1 - i

        @pl.when(target != me)
        def _():
            kv_copy(target, me).start()

        return c

    lax.fori_loop(0, n - base, send_kv, 0)
    for d in (2, 3, 1):
        qg_copy(1, 0, d, True).start()

    loads[3].wait()
    for c in range(CHUNKS):
        for d in (2, 3, 1, 0):
            peer = peer_of(d)
            cols = pl.ds(pl.multiple_of(peer * GW + c * hc * HD, hc * HD), hc * HD)
            part = dot(sel, q_in[:, cols], 1, 0).astype(BF)
            for h in range(hc):
                piece = part[:, h * HD:(h + 1) * HD]
                if d == 0:
                    q_recv[c * hc + h, mine] = piece
                else:
                    q_send[peer * GROUP + c * hc + h] = piece
            if d != 0:
                qg_copy(0, c, d, True).start()
                if c + 1 < CHUNKS:
                    qg_copy(1, c + 1, d, True).start()
    for h in range(GROUP):
        g_recv[h, mine] = g_send[mine * GROUP + h]

    def wait_kv(s, c):
        @pl.when(s != me)
        def _():
            kv_copy(s, s).wait_recv()

        return c

    lax.fori_loop(0, base + QUAD, wait_kv, 0)

    kv = kv_recv[...].reshape(keys, 2 * HD)
    k_all, v_all = kv[:, :HD], kv[:, HD:]
    crows = hc * span
    row_pos = base * keep + lax.broadcasted_iota(jnp.int32, (crows, keys), 0) % span
    seen = row_pos >= lax.broadcasted_iota(jnp.int32, (crows, keys), 1)

    def dkv_copy(target, source):
        return remote(
            dkv_send.at[target], dkv_recv.at[source], dkv_ssem.at[target],
            dkv_rsem.at[source], target,
        )

    def send_dkv(t, c):
        @pl.when(t != me)
        def _():
            dkv_copy(t, me).start()

        return c

    def ad_copy(which, chunk, d, send):
        peer = peer_of(d)
        buf_s, buf_r = ((att_send, att_recv), (dqs_send, dqs_recv))[which]
        slot = mine if send else peer
        cols = pl.ds(chunk * hc * HD, hc * HD)
        return remote(
            buf_s.at[peer, :, cols], buf_r.at[slot, :, cols],
            ad_ssem.at[which, chunk, d], ad_rsem.at[which, chunk, slot], base + peer,
        )

    for c in range(CHUNKS):
        for d in (1, 2, 3):
            qg_copy(1, c, d, False).wait_recv()
            qg_copy(0, c, d, False).wait_recv()
        q_c = q_recv[c * hc:(c + 1) * hc].reshape(crows, HD)
        g_c = g_recv[c * hc:(c + 1) * hc].reshape(crows, HD)
        scores = jnp.where(seen, dot(q_c, k_all, 1, 1) * scale, -jnp.inf)
        top = jnp.max(scores, axis=1, keepdims=True)
        e = jnp.exp(scores - top)
        probs = e * (1.0 / jnp.sum(e, axis=1, keepdims=True))
        low = probs.astype(BF)
        att = dot(low, v_all, 1, 0).astype(BF)
        gdot = jnp.sum(g_c.astype(F32) * att.astype(F32), axis=1, keepdims=True)
        gprob = dot(g_c, v_all, 1, 1)
        ds = (probs * (gprob - gdot)).astype(BF)
        def give(which, val):
            buf = (att_send, dqs_send)[which]
            for h in range(hc):
                hcol = slice((c * hc + h) * HD, (c * hc + h + 1) * HD)
                for b in range(QUAD):
                    r0 = h * span + b * keep
                    buf[b, :, hcol] = val[r0:r0 + keep]
            for d in (2, 3, 1):
                ad_copy(which, c, d, True).start()

        give(0, att)
        if c < CHUNKS - 1:
            give(1, (dot(ds, k_all, 1, 0) * scale).astype(BF))
        dk_part = dot(ds, q_c, 0, 0)
        dv_part = dot(low, g_c, 0, 0)
        if c:
            dk_part += dk_acc[...]
            dv_part += dv_acc[...]
        if c < CHUNKS - 1:
            dk_acc[...] = dk_part
            dv_acc[...] = dv_part
        else:
            dkv_send[:, :, :HD] = (dk_part * scale).astype(BF).reshape(n, keep, HD)
            dkv_send[:, :, HD:] = dv_part.astype(BF).reshape(n, keep, HD)
            lax.fori_loop(0, base + QUAD, send_dkv, 0)
            give(1, (dot(ds, k_all, 1, 0) * scale).astype(BF))

    dkv_recv[me] = dkv_send[me]
    att_recv[mine] = att_send[mine]
    dqs_recv[mine] = dqs_send[mine]

    for d in (0, 1, 3, 2):
        peer = peer_of(d)
        cols = pl.ds(pl.multiple_of(peer * GW, GW), GW)
        if d:
            for c in range(CHUNKS):
                ad_copy(0, c, d, False).wait_recv()
                ad_copy(1, c, d, False).wait_recv()
        pltpu.make_async_copy(att_recv.at[peer], att_out.at[:, cols], out_sem.at[0, d]).start()
        pltpu.make_async_copy(dqs_recv.at[peer], dq_out.at[:, cols], out_sem.at[1, d]).start()

    def wait_dkv(s, c):
        @pl.when(s != me)
        def _():
            dkv_copy(s, s).wait_recv()

        return c

    lax.fori_loop(base, n, wait_dkv, 0)

    def add_quad(j, tot):
        return tuple(
            tot[g] + dkv_recv[j * QUAD + g].astype(F32) for g in range(KVH)
        )

    total = lax.fori_loop(
        quad, n // QUAD, add_quad, tuple(jnp.zeros((keep, 2 * HD), F32) for _ in range(KVH))
    )
    for g in range(KVH):
        dkv_kept[:, g * HD:(g + 1) * HD] = total[g][:, :HD].astype(BF)
        dkv_kept[:, (KVH + g) * HD:(KVH + g + 1) * HD] = total[g][:, HD:].astype(BF)
    last = [sel_copy, pltpu.make_async_copy(dkv_kept, dkv_out, out_sem.at[2, 1])]
    last[1].start()

    def drain_kv(t, c):
        @pl.when(t != me)
        def _():
            kv_copy(t, me).wait_send()

        return c

    lax.fori_loop(base, n, drain_kv, 0)

    def drain_dkv(t, c):
        @pl.when(t != me)
        def _():
            dkv_copy(t, me).wait_send()

        return c

    lax.fori_loop(0, base + QUAD, drain_dkv, 0)
    for d in (1, 2, 3):
        for w in (0, 1):
            for c in range(CHUNKS):
                qg_copy(w, c, d, True).wait_send()
                ad_copy(w, c, d, True).wait_send()
    for d in range(QUAD):
        peer = peer_of(d)
        cols = pl.ds(pl.multiple_of(peer * GW, GW), GW)
        pltpu.make_async_copy(att_recv.at[peer], att_out.at[:, cols], out_sem.at[0, d]).wait()
        pltpu.make_async_copy(dqs_recv.at[peer], dq_out.at[:, cols], out_sem.at[1, d]).wait()
    for cp in last:
        cp.wait()


def spread_kernel(
    att_in, dq_in, dkv_in, sel_in, att_out, dq_out, dk_out, dv_out,
    dq_kept, dkv_kept, sel_ref, dq_full, dk_full, dv_full, att_keep, in_sem, out_sem,
):
    kvw = KVH * HD
    loads = []
    for i, (src, dst) in enumerate(
        ((sel_in, sel_ref), (dq_in, dq_kept), (dkv_in, dkv_kept), (att_in, att_keep))
    ):
        cp = pltpu.make_async_copy(src, dst, in_sem.at[i])
        cp.start()
        loads.append(cp)
    loads[0].wait()
    loads[1].wait()
    sel = sel_ref[...]
    stores = []
    for i in range(QUAD):
        cols = slice(i * GW, (i + 1) * GW)
        dq_full[:, cols] = dot(sel, dq_kept[:, cols], 0, 0).astype(BF)
        stores.append(pltpu.make_async_copy(dq_full.at[:, cols], dq_out.at[:, cols], out_sem.at[i]))
        stores[-1].start()
    loads[2].wait()
    for i, (full, out) in enumerate(((dk_full, dk_out), (dv_full, dv_out))):
        full[...] = dot(sel, dkv_kept[:, i * kvw:(i + 1) * kvw], 0, 0).astype(BF)
        stores.append(pltpu.make_async_copy(full, out, out_sem.at[QUAD + i]))
        stores[-1].start()
    loads[3].wait()
    stores.append(pltpu.make_async_copy(att_keep, att_out, out_sem.at[QUAD + 2]))
    stores[-1].start()
    for cp in stores:
        cp.wait()


def body(query_rows, key_rows, value_rows, keep_rank, out_grad):
    n = lax.axis_size("seq")
    rows = query_rows.shape[0]
    keep = out_grad.shape[0]
    width = HEADS * HD
    kvw = KVH * HD
    any_spec = pl.BlockSpec(memory_space=pl.ANY)
    vmem = pl.BlockSpec(memory_space=pltpu.VMEM)
    dma = pltpu.SemaphoreType.DMA
    hbm = pl.BlockSpec(memory_space=pltpu.HBM)
    att, dq_kept, dkv_kept, sel = pl.pallas_call(
        functools.partial(kernel, n, keep),
        out_shape=(
            jax.ShapeDtypeStruct((keep, width), BF),
            jax.ShapeDtypeStruct((keep, width), BF),
            jax.ShapeDtypeStruct((keep, 2 * kvw), BF),
            jax.ShapeDtypeStruct((keep, rows), BF),
        ),
        in_specs=[hbm, hbm, hbm, vmem, hbm],
        out_specs=(any_spec,) * 4,
        scratch_shapes=[
            pltpu.VMEM((rows, width), BF),
            pltpu.VMEM((rows, kvw), BF),
            pltpu.VMEM((rows, kvw), BF),
            pltpu.VMEM((keep, width), BF),
            pltpu.VMEM((HEADS, keep, HD), BF),
            pltpu.VMEM((HEADS, keep, HD), BF),
            pltpu.VMEM((KVH, keep, 2 * HD), BF),
            pltpu.VMEM((GROUP, QUAD, keep, HD), BF),
            pltpu.VMEM((GROUP, QUAD, keep, HD), BF),
            pltpu.VMEM((n, keep, 2 * HD), BF),
            pltpu.VMEM((n, keep, 2 * HD), BF),
            pltpu.VMEM((n, keep, 2 * HD), BF),
            pltpu.VMEM((QUAD, keep, GW), BF),
            pltpu.VMEM((QUAD, keep, GW), BF),
            pltpu.VMEM((QUAD, keep, GW), BF),
            pltpu.VMEM((QUAD, keep, GW), BF),
            pltpu.VMEM((keep, 2 * kvw), BF),
            pltpu.VMEM((keep, rows), BF),
            pltpu.VMEM((n * keep, HD), F32),
            pltpu.VMEM((n * keep, HD), F32),
            dma((4,)),
            dma((3, QUAD)),
            dma((2, CHUNKS, QUAD)),
            dma((2, CHUNKS, QUAD)),
            dma((n,)),
            dma((n,)),
            dma((2, CHUNKS, QUAD)),
            dma((2, CHUNKS, QUAD)),
            dma((n,)),
            dma((n,)),
        ],
        compiler_params=pltpu.CompilerParams(
            collective_id=0, has_side_effects=True, vmem_limit_bytes=64 * 1024 * 1024
        ),
    )(query_rows, key_rows, value_rows, keep_rank, out_grad)
    return pl.pallas_call(
        spread_kernel,
        out_shape=(
            jax.ShapeDtypeStruct((keep, width), BF),
            jax.ShapeDtypeStruct((rows, width), BF),
            jax.ShapeDtypeStruct((rows, kvw), BF),
            jax.ShapeDtypeStruct((rows, kvw), BF),
        ),
        in_specs=[any_spec] * 4,
        out_specs=(hbm,) * 4,
        scratch_shapes=[
            pltpu.VMEM((keep, width), BF),
            pltpu.VMEM((keep, 2 * kvw), BF),
            pltpu.VMEM((keep, rows), BF),
            pltpu.VMEM((rows, width), BF),
            pltpu.VMEM((rows, kvw), BF),
            pltpu.VMEM((rows, kvw), BF),
            pltpu.VMEM((keep, width), BF),
            dma((4,)),
            dma((QUAD + 3,)),
        ],
        compiler_params=pltpu.CompilerParams(vmem_limit_bytes=64 * 1024 * 1024),
    )(att, dq_kept, dkv_kept, sel)


def solution(mesh):
    spec = P(("groups", "seq"), None)
    return jax.shard_map(
        body, mesh=mesh, in_specs=(spec,) * 5, out_specs=(spec,) * 4, check_vma=False
    )
```

```python
import functools

import jax
import jax.numpy as jnp
from jax import lax
from jax.experimental import pallas as pl
from jax.experimental.pallas import tpu as pltpu
from jax.sharding import PartitionSpec as P

HEADS = 32
KVH = 4
HD = 128
GROUP = HEADS // KVH
QUAD = KVH
GW = GROUP * HD
CHUNKS = 2
BF = jnp.bfloat16
F32 = jnp.float32
MESH = pl.DeviceIdType.MESH


def dot(a, b, ca, cb):
    return lax.dot_general(a, b, (((ca,), (cb,)), ((), ())), preferred_element_type=F32)


def kernel(
    n, keep, q_hbm, k_hbm, v_hbm, rank_ref, g_hbm, att_out, dq_out, dkv_out, sel_out,
    q_in, k_in, v_in, g_in, q_send, g_send, kv_send, q_recv, g_recv, kv_recv,
    dkv_send, dkv_recv, att_send, dqs_send, att_recv, dqs_recv, dkv_kept, sel_keep,
    dk_acc, dv_acc, in_sem, out_sem, qg_ssem, qg_rsem, kv_ssem, kv_rsem,
    ad_ssem, ad_rsem, dkv_ssem, dkv_rsem,
):
    rows = q_in.shape[0]
    me = lax.axis_index("seq")
    quad = me // QUAD
    mine = me % QUAD
    base = quad * QUAD
    keys = n * keep
    scale = HD ** -0.5
    hc = GROUP // CHUNKS
    span = QUAD * keep

    def peer_of(d):
        return (mine // 2 + d // 2) % 2 * 2 + (mine + d) % 2

    barrier = pltpu.get_barrier_semaphore()

    def greet(off, c):
        pl.semaphore_signal(
            barrier, inc=1, device_id={"seq": lax.rem(me + off, n)}, device_id_type=MESH
        )
        return c

    lax.fori_loop(1, n, greet, 0)

    loads = []
    for i, (src, dst) in enumerate(((k_hbm, k_in), (v_hbm, v_in), (g_hbm, g_in), (q_hbm, q_in))):
        cp = pltpu.make_async_copy(src, dst, in_sem.at[i])
        cp.start()
        loads.append(cp)

    def remote(src, dst, ssem, rsem, target):
        return pltpu.make_async_remote_copy(
            src_ref=src, dst_ref=dst, send_sem=ssem, recv_sem=rsem,
            device_id={"seq": target}, device_id_type=MESH,
        )

    chosen = rank_ref[...] < keep
    chosen_low = jnp.broadcast_to(jnp.where(chosen, 1.0, 0.0).astype(F32), (8, rows)).astype(BF)
    upto = (
        lax.broadcasted_iota(jnp.int32, (rows, rows), 0)
        <= lax.broadcasted_iota(jnp.int32, (rows, rows), 1)
    )
    slots = dot(chosen_low, jnp.where(upto, 1.0, 0.0).astype(BF), 1, 0)[0:1]
    slots = jnp.where(chosen, slots, 0.0)
    wanted = lax.broadcasted_iota(jnp.int32, (keep, rows), 0).astype(F32) + 1.0
    sel = jnp.where(wanted == slots, 1.0, 0.0).astype(BF)
    sel_keep[...] = sel
    sel_copy = pltpu.make_async_copy(sel_keep, sel_out, out_sem.at[2, 0])
    sel_copy.start()

    loads[0].wait()
    loads[1].wait()
    k_kept = dot(sel, k_in[...], 1, 0).astype(BF)
    v_kept = dot(sel, v_in[...], 1, 0).astype(BF)
    for g in range(KVH):
        kv_send[g, :, :HD] = k_kept[:, g * HD:(g + 1) * HD]
        kv_send[g, :, HD:] = v_kept[:, g * HD:(g + 1) * HD]
    kv_recv[me] = kv_send[mine]

    def clear(s, c):
        kv_recv[s] = jnp.zeros((keep, 2 * HD), BF)
        return c

    lax.fori_loop(base + QUAD, n, clear, 0)

    loads[2].wait()
    for h in range(HEADS):
        g_send[h] = g_in[:, h * HD:(h + 1) * HD]

    pl.semaphore_wait(barrier, n - 1)

    def kv_copy(target, source):
        return remote(
            kv_send.at[target % QUAD], kv_recv.at[source], kv_ssem.at[target],
            kv_rsem.at[source], target,
        )

    def qg_copy(which, c, d, send):
        peer = peer_of(d)
        buf_s, buf_r = ((q_send, q_recv), (g_send, g_recv))[which]
        return remote(
            buf_s.at[pl.ds(peer * GROUP + c * hc, hc)],
            buf_r.at[pl.ds(c * hc, hc), mine if send else peer],
            qg_ssem.at[which, c, d], qg_rsem.at[which, c, mine if send else peer], base + peer,
        )

    def send_kv(i, c):
        target = n - 1 - i

        @pl.when(target != me)
        def _():
            kv_copy(target, me).start()

        return c

    for d in (2, 3, 1):
        qg_copy(1, 0, d, True).start()
    lax.fori_loop(0, n - base, send_kv, 0)

    loads[3].wait()
    for c in range(CHUNKS):
        for d in (2, 3, 1, 0):
            peer = peer_of(d)
            cols = pl.ds(pl.multiple_of(peer * GW + c * hc * HD, hc * HD), hc * HD)
            part = dot(sel, q_in[:, cols], 1, 0).astype(BF)
            for h in range(hc):
                piece = part[:, h * HD:(h + 1) * HD]
                if d == 0:
                    q_recv[c * hc + h, mine] = piece
                else:
                    q_send[peer * GROUP + c * hc + h] = piece
            if d != 0:
                qg_copy(0, c, d, True).start()
                if c + 1 < CHUNKS:
                    qg_copy(1, c + 1, d, True).start()
    for h in range(GROUP):
        g_recv[h, mine] = g_send[mine * GROUP + h]

    def wait_kv(s, c):
        @pl.when(s != me)
        def _():
            kv_copy(s, s).wait_recv()

        return c

    lax.fori_loop(0, base + QUAD, wait_kv, 0)

    kv = kv_recv[...].reshape(keys, 2 * HD)
    k_all, v_all = kv[:, :HD], kv[:, HD:]
    crows = hc * span
    row_pos = base * keep + lax.broadcasted_iota(jnp.int32, (crows, keys), 0) % span
    seen = row_pos >= lax.broadcasted_iota(jnp.int32, (crows, keys), 1)

    def dkv_copy(target, source):
        return remote(
            dkv_send.at[target], dkv_recv.at[source], dkv_ssem.at[target],
            dkv_rsem.at[source], target,
        )

    def send_dkv(t, c):
        @pl.when(t != me)
        def _():
            dkv_copy(t, me).start()

        return c

    def ad_copy(which, chunk, d, send):
        peer = peer_of(d)
        buf_s, buf_r = ((att_send, att_recv), (dqs_send, dqs_recv))[which]
        slot = mine if send else peer
        cols = pl.ds(chunk * hc * HD, hc * HD)
        return remote(
            buf_s.at[peer, :, cols], buf_r.at[slot, :, cols],
            ad_ssem.at[which, chunk, d], ad_rsem.at[which, chunk, slot], base + peer,
        )

    for c in range(CHUNKS):
        for d in (1, 2, 3):
            qg_copy(1, c, d, False).wait_recv()
            qg_copy(0, c, d, False).wait_recv()
        q_c = q_recv[c * hc:(c + 1) * hc].reshape(crows, HD)
        g_c = g_recv[c * hc:(c + 1) * hc].reshape(crows, HD)
        scores = jnp.where(seen, dot(q_c, k_all, 1, 1) * scale, -jnp.inf)
        top = jnp.max(scores, axis=1, keepdims=True)
        e = jnp.exp(scores - top)
        probs = e * (1.0 / jnp.sum(e, axis=1, keepdims=True))
        low = probs.astype(BF)
        att = dot(low, v_all, 1, 0).astype(BF)
        gdot = jnp.sum(g_c.astype(F32) * att.astype(F32), axis=1, keepdims=True)
        gprob = dot(g_c, v_all, 1, 1)
        ds = (probs * (gprob - gdot)).astype(BF)
        def give(which, val):
            buf = (att_send, dqs_send)[which]
            for h in range(hc):
                hcol = slice((c * hc + h) * HD, (c * hc + h + 1) * HD)
                for b in range(QUAD):
                    r0 = h * span + b * keep
                    buf[b, :, hcol] = val[r0:r0 + keep]
            for d in (2, 3, 1):
                ad_copy(which, c, d, True).start()

        give(0, att)
        if c < CHUNKS - 1:
            give(1, (dot(ds, k_all, 1, 0) * scale).astype(BF))
        dk_part = dot(ds, q_c, 0, 0)
        dv_part = dot(low, g_c, 0, 0)
        if c:
            dk_part += dk_acc[...]
            dv_part += dv_acc[...]
        if c < CHUNKS - 1:
            dk_acc[...] = dk_part
            dv_acc[...] = dv_part
        else:
            dkv_send[:, :, :HD] = (dk_part * scale).astype(BF).reshape(n, keep, HD)
            dkv_send[:, :, HD:] = dv_part.astype(BF).reshape(n, keep, HD)
            lax.fori_loop(0, base + QUAD, send_dkv, 0)
            give(1, (dot(ds, k_all, 1, 0) * scale).astype(BF))

    dkv_recv[me] = dkv_send[me]
    att_recv[mine] = att_send[mine]
    dqs_recv[mine] = dqs_send[mine]

    for d in (0, 1, 3, 2):
        peer = peer_of(d)
        cols = pl.ds(pl.multiple_of(peer * GW, GW), GW)
        if d:
            for c in range(CHUNKS):
                ad_copy(0, c, d, False).wait_recv()
                ad_copy(1, c, d, False).wait_recv()
        pltpu.make_async_copy(att_recv.at[peer], att_out.at[:, cols], out_sem.at[0, d]).start()
        pltpu.make_async_copy(dqs_recv.at[peer], dq_out.at[:, cols], out_sem.at[1, d]).start()

    def wait_dkv(s, c):
        @pl.when(s != me)
        def _():
            dkv_copy(s, s).wait_recv()

        return c

    def add_quad(j, tot):
        lax.fori_loop(j * QUAD, j * QUAD + QUAD, wait_dkv, 0)
        return tuple(
            tot[g] + dkv_recv[j * QUAD + g].astype(F32) for g in range(KVH)
        )

    total = lax.fori_loop(
        quad, n // QUAD, add_quad, tuple(jnp.zeros((keep, 2 * HD), F32) for _ in range(KVH))
    )
    for g in range(KVH):
        dkv_kept[:, g * HD:(g + 1) * HD] = total[g][:, :HD].astype(BF)
        dkv_kept[:, (KVH + g) * HD:(KVH + g + 1) * HD] = total[g][:, HD:].astype(BF)
    last = [sel_copy, pltpu.make_async_copy(dkv_kept, dkv_out, out_sem.at[2, 1])]
    last[1].start()

    def drain_kv(t, c):
        @pl.when(t != me)
        def _():
            kv_copy(t, me).wait_send()

        return c

    lax.fori_loop(base, n, drain_kv, 0)

    def drain_dkv(t, c):
        @pl.when(t != me)
        def _():
            dkv_copy(t, me).wait_send()

        return c

    lax.fori_loop(0, base + QUAD, drain_dkv, 0)
    for d in (1, 2, 3):
        for w in (0, 1):
            for c in range(CHUNKS):
                qg_copy(w, c, d, True).wait_send()
                ad_copy(w, c, d, True).wait_send()
    for d in range(QUAD):
        peer = peer_of(d)
        cols = pl.ds(pl.multiple_of(peer * GW, GW), GW)
        pltpu.make_async_copy(att_recv.at[peer], att_out.at[:, cols], out_sem.at[0, d]).wait()
        pltpu.make_async_copy(dqs_recv.at[peer], dq_out.at[:, cols], out_sem.at[1, d]).wait()
    for cp in last:
        cp.wait()


def spread_kernel(
    att_in, dq_in, dkv_in, sel_in, att_out, dq_out, dk_out, dv_out,
    dq_kept, dkv_kept, sel_ref, dq_full, dk_full, dv_full, att_keep, in_sem, out_sem,
):
    kvw = KVH * HD
    loads = []
    for i, (src, dst) in enumerate(
        ((sel_in, sel_ref), (dq_in, dq_kept), (dkv_in, dkv_kept), (att_in, att_keep))
    ):
        cp = pltpu.make_async_copy(src, dst, in_sem.at[i])
        cp.start()
        loads.append(cp)
    loads[0].wait()
    loads[1].wait()
    sel = sel_ref[...]
    stores = []
    for i in range(QUAD):
        cols = slice(i * GW, (i + 1) * GW)
        dq_full[:, cols] = dot(sel, dq_kept[:, cols], 0, 0).astype(BF)
        stores.append(pltpu.make_async_copy(dq_full.at[:, cols], dq_out.at[:, cols], out_sem.at[i]))
        stores[-1].start()
    loads[2].wait()
    for i, (full, out) in enumerate(((dk_full, dk_out), (dv_full, dv_out))):
        full[...] = dot(sel, dkv_kept[:, i * kvw:(i + 1) * kvw], 0, 0).astype(BF)
        stores.append(pltpu.make_async_copy(full, out, out_sem.at[QUAD + i]))
        stores[-1].start()
    loads[3].wait()
    stores.append(pltpu.make_async_copy(att_keep, att_out, out_sem.at[QUAD + 2]))
    stores[-1].start()
    for cp in stores:
        cp.wait()


def body(query_rows, key_rows, value_rows, keep_rank, out_grad):
    n = lax.axis_size("seq")
    rows = query_rows.shape[0]
    keep = out_grad.shape[0]
    width = HEADS * HD
    kvw = KVH * HD
    any_spec = pl.BlockSpec(memory_space=pl.ANY)
    vmem = pl.BlockSpec(memory_space=pltpu.VMEM)
    dma = pltpu.SemaphoreType.DMA
    hbm = pl.BlockSpec(memory_space=pltpu.HBM)
    att, dq_kept, dkv_kept, sel = pl.pallas_call(
        functools.partial(kernel, n, keep),
        out_shape=(
            jax.ShapeDtypeStruct((keep, width), BF),
            jax.ShapeDtypeStruct((keep, width), BF),
            jax.ShapeDtypeStruct((keep, 2 * kvw), BF),
            jax.ShapeDtypeStruct((keep, rows), BF),
        ),
        in_specs=[hbm, hbm, hbm, vmem, hbm],
        out_specs=(any_spec,) * 4,
        scratch_shapes=[
            pltpu.VMEM((rows, width), BF),
            pltpu.VMEM((rows, kvw), BF),
            pltpu.VMEM((rows, kvw), BF),
            pltpu.VMEM((keep, width), BF),
            pltpu.VMEM((HEADS, keep, HD), BF),
            pltpu.VMEM((HEADS, keep, HD), BF),
            pltpu.VMEM((KVH, keep, 2 * HD), BF),
            pltpu.VMEM((GROUP, QUAD, keep, HD), BF),
            pltpu.VMEM((GROUP, QUAD, keep, HD), BF),
            pltpu.VMEM((n, keep, 2 * HD), BF),
            pltpu.VMEM((n, keep, 2 * HD), BF),
            pltpu.VMEM((n, keep, 2 * HD), BF),
            pltpu.VMEM((QUAD, keep, GW), BF),
            pltpu.VMEM((QUAD, keep, GW), BF),
            pltpu.VMEM((QUAD, keep, GW), BF),
            pltpu.VMEM((QUAD, keep, GW), BF),
            pltpu.VMEM((keep, 2 * kvw), BF),
            pltpu.VMEM((keep, rows), BF),
            pltpu.VMEM((n * keep, HD), F32),
            pltpu.VMEM((n * keep, HD), F32),
            dma((4,)),
            dma((3, QUAD)),
            dma((2, CHUNKS, QUAD)),
            dma((2, CHUNKS, QUAD)),
            dma((n,)),
            dma((n,)),
            dma((2, CHUNKS, QUAD)),
            dma((2, CHUNKS, QUAD)),
            dma((n,)),
            dma((n,)),
        ],
        compiler_params=pltpu.CompilerParams(
            collective_id=0, has_side_effects=True, vmem_limit_bytes=64 * 1024 * 1024
        ),
    )(query_rows, key_rows, value_rows, keep_rank, out_grad)
    return pl.pallas_call(
        spread_kernel,
        out_shape=(
            jax.ShapeDtypeStruct((keep, width), BF),
            jax.ShapeDtypeStruct((rows, width), BF),
            jax.ShapeDtypeStruct((rows, kvw), BF),
            jax.ShapeDtypeStruct((rows, kvw), BF),
        ),
        in_specs=[any_spec] * 4,
        out_specs=(hbm,) * 4,
        scratch_shapes=[
            pltpu.VMEM((keep, width), BF),
            pltpu.VMEM((keep, 2 * kvw), BF),
            pltpu.VMEM((keep, rows), BF),
            pltpu.VMEM((rows, width), BF),
            pltpu.VMEM((rows, kvw), BF),
            pltpu.VMEM((rows, kvw), BF),
            pltpu.VMEM((keep, width), BF),
            dma((4,)),
            dma((QUAD + 3,)),
        ],
        compiler_params=pltpu.CompilerParams(vmem_limit_bytes=64 * 1024 * 1024),
    )(att, dq_kept, dkv_kept, sel)


def solution(mesh):
    spec = P(("groups", "seq"), None)
    return jax.shard_map(
        body, mesh=mesh, in_specs=(spec,) * 5, out_specs=(spec,) * 4, check_vma=False
    )
```

```python
import functools

import jax
import jax.numpy as jnp
from jax import lax
from jax.experimental import pallas as pl
from jax.experimental.pallas import tpu as pltpu
from jax.sharding import PartitionSpec as P

HEADS = 32
KVH = 4
HD = 128
GROUP = HEADS // KVH
QUAD = KVH
GW = GROUP * HD
CHUNKS = 2
PIECES = 8
PW = HEADS * HD // PIECES
BF = jnp.bfloat16
F32 = jnp.float32
MESH = pl.DeviceIdType.MESH


def dot(a, b, ca, cb):
    return lax.dot_general(a, b, (((ca,), (cb,)), ((), ())), preferred_element_type=F32)


def kernel(
    n, keep, q_hbm, k_hbm, v_hbm, rank_ref, g_hbm, att_out, dq_out, dkv_out, sel_out,
    q_in, k_in, v_in, g_in, q_send, g_send, kv_send, q_recv, g_recv, kv_recv,
    dkv_send, dkv_recv, att_send, dqs_send, att_recv, dqs_recv, dkv_kept, sel_keep,
    dk_acc, dv_acc, in_sem, out_sem, qg_ssem, qg_rsem, kv_ssem, kv_rsem,
    ad_ssem, ad_rsem, dkv_ssem, dkv_rsem,
):
    rows = q_in.shape[0]
    me = lax.axis_index("seq")
    quad = me // QUAD
    mine = me % QUAD
    base = quad * QUAD
    keys = n * keep
    scale = HD ** -0.5
    hc = GROUP // CHUNKS
    span = QUAD * keep

    def peer_of(d):
        return (mine // 2 + d // 2) % 2 * 2 + (mine + d) % 2

    barrier = pltpu.get_barrier_semaphore()

    def greet(off, c):
        pl.semaphore_signal(
            barrier, inc=1, device_id={"seq": lax.rem(me + off, n)}, device_id_type=MESH
        )
        return c

    lax.fori_loop(1, n, greet, 0)

    loads = []
    for i, (src, dst) in enumerate(((k_hbm, k_in), (v_hbm, v_in), (g_hbm, g_in), (q_hbm, q_in))):
        cp = pltpu.make_async_copy(src, dst, in_sem.at[i])
        cp.start()
        loads.append(cp)

    def remote(src, dst, ssem, rsem, target):
        return pltpu.make_async_remote_copy(
            src_ref=src, dst_ref=dst, send_sem=ssem, recv_sem=rsem,
            device_id={"seq": target}, device_id_type=MESH,
        )

    chosen = rank_ref[...] < keep
    chosen_low = jnp.broadcast_to(jnp.where(chosen, 1.0, 0.0).astype(F32), (8, rows)).astype(BF)
    upto = (
        lax.broadcasted_iota(jnp.int32, (rows, rows), 0)
        <= lax.broadcasted_iota(jnp.int32, (rows, rows), 1)
    )
    slots = dot(chosen_low, jnp.where(upto, 1.0, 0.0).astype(BF), 1, 0)[0:1]
    slots = jnp.where(chosen, slots, 0.0)
    wanted = lax.broadcasted_iota(jnp.int32, (keep, rows), 0).astype(F32) + 1.0
    sel = jnp.where(wanted == slots, 1.0, 0.0).astype(BF)
    sel_keep[...] = sel
    sel_copy = pltpu.make_async_copy(sel_keep, sel_out, out_sem.at[2, 0])
    sel_copy.start()

    loads[0].wait()
    loads[1].wait()
    k_kept = dot(sel, k_in[...], 1, 0).astype(BF)
    v_kept = dot(sel, v_in[...], 1, 0).astype(BF)
    for g in range(KVH):
        kv_send[g, :, :HD] = k_kept[:, g * HD:(g + 1) * HD]
        kv_send[g, :, HD:] = v_kept[:, g * HD:(g + 1) * HD]
    kv_recv[me] = kv_send[mine]

    def clear(s, c):
        kv_recv[s] = jnp.zeros((keep, 2 * HD), BF)
        return c

    lax.fori_loop(base + QUAD, n, clear, 0)

    loads[2].wait()
    for h in range(HEADS):
        g_send[h] = g_in[:, h * HD:(h + 1) * HD]

    pl.semaphore_wait(barrier, n - 1)

    def kv_copy(target, source):
        return remote(
            kv_send.at[target % QUAD], kv_recv.at[source], kv_ssem.at[target],
            kv_rsem.at[source], target,
        )

    def qg_copy(which, c, d, send):
        peer = peer_of(d)
        buf_s, buf_r = ((q_send, q_recv), (g_send, g_recv))[which]
        return remote(
            buf_s.at[pl.ds(peer * GROUP + c * hc, hc)],
            buf_r.at[pl.ds(c * hc, hc), mine if send else peer],
            qg_ssem.at[which, c, d], qg_rsem.at[which, c, mine if send else peer], base + peer,
        )

    def send_kv(i, c):
        target = n - 1 - i

        @pl.when(target != me)
        def _():
            kv_copy(target, me).start()

        return c

    for d in (2, 3, 1):
        qg_copy(1, 0, d, True).start()
    lax.fori_loop(0, n - base, send_kv, 0)

    loads[3].wait()
    for c in range(CHUNKS):
        for d in (2, 3, 1, 0):
            peer = peer_of(d)
            cols = pl.ds(pl.multiple_of(peer * GW + c * hc * HD, hc * HD), hc * HD)
            part = dot(sel, q_in[:, cols], 1, 0).astype(BF)
            for h in range(hc):
                piece = part[:, h * HD:(h + 1) * HD]
                if d == 0:
                    q_recv[c * hc + h, mine] = piece
                else:
                    q_send[peer * GROUP + c * hc + h] = piece
            if d != 0:
                qg_copy(0, c, d, True).start()
                if c + 1 < CHUNKS:
                    qg_copy(1, c + 1, d, True).start()
    for h in range(GROUP):
        g_recv[h, mine] = g_send[mine * GROUP + h]

    def wait_kv(s, c):
        @pl.when(s != me)
        def _():
            kv_copy(s, s).wait_recv()

        return c

    lax.fori_loop(0, base + QUAD, wait_kv, 0)

    kv = kv_recv[...].reshape(keys, 2 * HD)
    k_all, v_all = kv[:, :HD], kv[:, HD:]
    crows = hc * span
    row_pos = base * keep + lax.broadcasted_iota(jnp.int32, (crows, keys), 0) % span
    seen = row_pos >= lax.broadcasted_iota(jnp.int32, (crows, keys), 1)

    def dkv_copy(target, source):
        return remote(
            dkv_send.at[target], dkv_recv.at[source], dkv_ssem.at[target],
            dkv_rsem.at[source], target,
        )

    def send_dkv(t, c):
        @pl.when(t != me)
        def _():
            dkv_copy(t, me).start()

        return c

    def ad_copy(which, chunk, d, send):
        peer = peer_of(d)
        buf_s, buf_r = ((att_send, att_recv), (dqs_send, dqs_recv))[which]
        slot = mine if send else peer
        cols = pl.ds(chunk * hc * HD, hc * HD)
        return remote(
            buf_s.at[peer, :, cols], buf_r.at[slot, :, cols],
            ad_ssem.at[which, chunk, d], ad_rsem.at[which, chunk, slot], base + peer,
        )

    for c in range(CHUNKS):
        for d in (1, 2, 3):
            qg_copy(1, c, d, False).wait_recv()
            qg_copy(0, c, d, False).wait_recv()
        q_c = q_recv[c * hc:(c + 1) * hc].reshape(crows, HD)
        g_c = g_recv[c * hc:(c + 1) * hc].reshape(crows, HD)
        scores = jnp.where(seen, dot(q_c, k_all, 1, 1) * scale, -jnp.inf)
        top = jnp.max(scores, axis=1, keepdims=True)
        e = jnp.exp(scores - top)
        probs = e * (1.0 / jnp.sum(e, axis=1, keepdims=True))
        low = probs.astype(BF)
        att = dot(low, v_all, 1, 0).astype(BF)
        gdot = jnp.sum(g_c.astype(F32) * att.astype(F32), axis=1, keepdims=True)
        gprob = dot(g_c, v_all, 1, 1)
        ds = (probs * (gprob - gdot)).astype(BF)
        def give(which, val):
            buf = (att_send, dqs_send)[which]
            for h in range(hc):
                hcol = slice((c * hc + h) * HD, (c * hc + h + 1) * HD)
                for b in range(QUAD):
                    r0 = h * span + b * keep
                    buf[b, :, hcol] = val[r0:r0 + keep]
            for d in (2, 3, 1):
                ad_copy(which, c, d, True).start()

        give(0, att)
        if c < CHUNKS - 1:
            give(1, (dot(ds, k_all, 1, 0) * scale).astype(BF))
        dk_part = dot(ds, q_c, 0, 0)
        dv_part = dot(low, g_c, 0, 0)
        if c:
            dk_part += dk_acc[...]
            dv_part += dv_acc[...]
        if c < CHUNKS - 1:
            dk_acc[...] = dk_part
            dv_acc[...] = dv_part
        else:
            dkv_send[:, :, :HD] = (dk_part * scale).astype(BF).reshape(n, keep, HD)
            dkv_send[:, :, HD:] = dv_part.astype(BF).reshape(n, keep, HD)
            lax.fori_loop(0, base + QUAD, send_dkv, 0)
            give(1, (dot(ds, k_all, 1, 0) * scale).astype(BF))

    dkv_recv[me] = dkv_send[me]
    att_recv[mine] = att_send[mine]
    dqs_recv[mine] = dqs_send[mine]

    for d in (0, 1, 3, 2):
        peer = peer_of(d)
        cols = pl.ds(pl.multiple_of(peer * GW, GW), GW)
        if d:
            for c in range(CHUNKS):
                ad_copy(0, c, d, False).wait_recv()
                ad_copy(1, c, d, False).wait_recv()
        pltpu.make_async_copy(att_recv.at[peer], att_out.at[:, cols], out_sem.at[0, d]).start()
        pltpu.make_async_copy(dqs_recv.at[peer], dq_out.at[:, cols], out_sem.at[1, d]).start()

    def wait_dkv(s, c):
        @pl.when(s != me)
        def _():
            dkv_copy(s, s).wait_recv()

        return c

    def add_quad(j, tot):
        lax.fori_loop(j * QUAD, j * QUAD + QUAD, wait_dkv, 0)
        return tuple(
            tot[g] + dkv_recv[j * QUAD + g].astype(F32) for g in range(KVH)
        )

    total = lax.fori_loop(
        quad, n // QUAD, add_quad, tuple(jnp.zeros((keep, 2 * HD), F32) for _ in range(KVH))
    )
    for g in range(KVH):
        dkv_kept[:, g * HD:(g + 1) * HD] = total[g][:, :HD].astype(BF)
        dkv_kept[:, (KVH + g) * HD:(KVH + g + 1) * HD] = total[g][:, HD:].astype(BF)
    last = [sel_copy, pltpu.make_async_copy(dkv_kept, dkv_out, out_sem.at[2, 1])]
    last[1].start()

    def drain_kv(t, c):
        @pl.when(t != me)
        def _():
            kv_copy(t, me).wait_send()

        return c

    lax.fori_loop(base, n, drain_kv, 0)

    def drain_dkv(t, c):
        @pl.when(t != me)
        def _():
            dkv_copy(t, me).wait_send()

        return c

    lax.fori_loop(0, base + QUAD, drain_dkv, 0)
    for d in (1, 2, 3):
        for w in (0, 1):
            for c in range(CHUNKS):
                qg_copy(w, c, d, True).wait_send()
                ad_copy(w, c, d, True).wait_send()
    for d in range(QUAD):
        peer = peer_of(d)
        cols = pl.ds(pl.multiple_of(peer * GW, GW), GW)
        pltpu.make_async_copy(att_recv.at[peer], att_out.at[:, cols], out_sem.at[0, d]).wait()
        pltpu.make_async_copy(dqs_recv.at[peer], dq_out.at[:, cols], out_sem.at[1, d]).wait()
    for cp in last:
        cp.wait()


def spread_kernel(
    att_in, dq_in, dkv_in, sel_in, att_out, dq_out, dk_out, dv_out,
    dq_kept, dkv_kept, sel_ref, dq_full, dk_full, dv_full, att_keep, in_sem, out_sem,
):
    kvw = KVH * HD
    loads = []
    for i, (src, dst) in enumerate(
        ((sel_in, sel_ref), (dq_in, dq_kept), (dkv_in, dkv_kept), (att_in, att_keep))
    ):
        cp = pltpu.make_async_copy(src, dst, in_sem.at[i])
        cp.start()
        loads.append(cp)
    loads[0].wait()
    loads[1].wait()
    sel = sel_ref[...]
    stores = []
    for i in range(PIECES):
        cols = slice(i * PW, (i + 1) * PW)
        dq_full[:, cols] = dot(sel, dq_kept[:, cols], 0, 0).astype(BF)
        stores.append(pltpu.make_async_copy(dq_full.at[:, cols], dq_out.at[:, cols], out_sem.at[i]))
        stores[-1].start()
    loads[2].wait()
    for i, (full, out) in enumerate(((dk_full, dk_out), (dv_full, dv_out))):
        full[...] = dot(sel, dkv_kept[:, i * kvw:(i + 1) * kvw], 0, 0).astype(BF)
        stores.append(pltpu.make_async_copy(full, out, out_sem.at[PIECES + i]))
        stores[-1].start()
    loads[3].wait()
    stores.append(pltpu.make_async_copy(att_keep, att_out, out_sem.at[PIECES + 2]))
    stores[-1].start()
    for cp in stores:
        cp.wait()


def body(query_rows, key_rows, value_rows, keep_rank, out_grad):
    n = lax.axis_size("seq")
    rows = query_rows.shape[0]
    keep = out_grad.shape[0]
    width = HEADS * HD
    kvw = KVH * HD
    any_spec = pl.BlockSpec(memory_space=pl.ANY)
    vmem = pl.BlockSpec(memory_space=pltpu.VMEM)
    dma = pltpu.SemaphoreType.DMA
    hbm = pl.BlockSpec(memory_space=pltpu.HBM)
    att, dq_kept, dkv_kept, sel = pl.pallas_call(
        functools.partial(kernel, n, keep),
        out_shape=(
            jax.ShapeDtypeStruct((keep, width), BF),
            jax.ShapeDtypeStruct((keep, width), BF),
            jax.ShapeDtypeStruct((keep, 2 * kvw), BF),
            jax.ShapeDtypeStruct((keep, rows), BF),
        ),
        in_specs=[hbm, hbm, hbm, vmem, hbm],
        out_specs=(any_spec,) * 4,
        scratch_shapes=[
            pltpu.VMEM((rows, width), BF),
            pltpu.VMEM((rows, kvw), BF),
            pltpu.VMEM((rows, kvw), BF),
            pltpu.VMEM((keep, width), BF),
            pltpu.VMEM((HEADS, keep, HD), BF),
            pltpu.VMEM((HEADS, keep, HD), BF),
            pltpu.VMEM((KVH, keep, 2 * HD), BF),
            pltpu.VMEM((GROUP, QUAD, keep, HD), BF),
            pltpu.VMEM((GROUP, QUAD, keep, HD), BF),
            pltpu.VMEM((n, keep, 2 * HD), BF),
            pltpu.VMEM((n, keep, 2 * HD), BF),
            pltpu.VMEM((n, keep, 2 * HD), BF),
            pltpu.VMEM((QUAD, keep, GW), BF),
            pltpu.VMEM((QUAD, keep, GW), BF),
            pltpu.VMEM((QUAD, keep, GW), BF),
            pltpu.VMEM((QUAD, keep, GW), BF),
            pltpu.VMEM((keep, 2 * kvw), BF),
            pltpu.VMEM((keep, rows), BF),
            pltpu.VMEM((n * keep, HD), F32),
            pltpu.VMEM((n * keep, HD), F32),
            dma((4,)),
            dma((3, QUAD)),
            dma((2, CHUNKS, QUAD)),
            dma((2, CHUNKS, QUAD)),
            dma((n,)),
            dma((n,)),
            dma((2, CHUNKS, QUAD)),
            dma((2, CHUNKS, QUAD)),
            dma((n,)),
            dma((n,)),
        ],
        compiler_params=pltpu.CompilerParams(
            collective_id=0, has_side_effects=True, vmem_limit_bytes=64 * 1024 * 1024
        ),
    )(query_rows, key_rows, value_rows, keep_rank, out_grad)
    return pl.pallas_call(
        spread_kernel,
        out_shape=(
            jax.ShapeDtypeStruct((keep, width), BF),
            jax.ShapeDtypeStruct((rows, width), BF),
            jax.ShapeDtypeStruct((rows, kvw), BF),
            jax.ShapeDtypeStruct((rows, kvw), BF),
        ),
        in_specs=[any_spec] * 4,
        out_specs=(hbm,) * 4,
        scratch_shapes=[
            pltpu.VMEM((keep, width), BF),
            pltpu.VMEM((keep, 2 * kvw), BF),
            pltpu.VMEM((keep, rows), BF),
            pltpu.VMEM((rows, width), BF),
            pltpu.VMEM((rows, kvw), BF),
            pltpu.VMEM((rows, kvw), BF),
            pltpu.VMEM((keep, width), BF),
            dma((4,)),
            dma((PIECES + 3,)),
        ],
        compiler_params=pltpu.CompilerParams(vmem_limit_bytes=64 * 1024 * 1024),
    )(att, dq_kept, dkv_kept, sel)


def solution(mesh):
    spec = P(("groups", "seq"), None)
    return jax.shard_map(
        body, mesh=mesh, in_specs=(spec,) * 5, out_specs=(spec,) * 4, check_vma=False
    )
```
